32 devices in a mesh: dp: 4 (over z), row: 2 (over y), col: 4 (over x, core).
Axes of the slice: x: 2, y: 2, z: 4, core: 2. Of those that a mesh axis runs over, the one named last changes fastest.
Arguments:
- hidden_in: bfloat16 [32768, 960], P(('dp', 'row', 'col')), may hold values from -30 to 30
- cotangent: bfloat16 [32768, 960], P(('dp', 'row', 'col')), may hold values from -6 to 6
- segment_ids: int32 [32768], P(('dp', 'row', 'col')), may hold values from 0 to 6, as said below
- positions: int32 [32768], P(('dp', 'row', 'col')), may hold values from 0 to 2047, as said below
- query_weight: float32 [960, 960], P('row', 'col'), may hold values from -0.1875 to 0.1875
- key_weight: float32 [960, 320], P('row', 'col'), may hold values from -0.1875 to 0.1875
- value_weight: float32 [960, 320], P('row', 'col'), may hold values from -0.1875 to 0.1875
- output_weight: float32 [960, 960], P('row', 'col'), may hold values from -0.75 to 0.75
- gate_up_weight: float32 [2, 960, 2560], P(None, 'row', 'col'), may hold values from -0.1875 to 0.1875
- down_weight: float32 [960, 2560], P('row', 'col'), may hold values from -0.125 to 0.125
- norm_gains: float32 [2, 960], replicated, may hold values from 0.5 to 1.5
- query_moment: float32 [960, 960], P('row', 'col'), may hold values from -256 to 256
- key_moment: float32 [960, 320], P('row', 'col'), may hold values from -256 to 256
- value_moment: float32 [960, 320], P('row', 'col'), may hold values from -256 to 256
- output_moment: float32 [960, 960], P('row', 'col'), may hold values from -64 to 64
- gate_up_moment: float32 [2, 960, 2560], P(None, 'row', 'col'), may hold values from -64 to 64
- down_moment: float32 [960, 2560], P('row', 'col'), may hold values from -128 to 128
- gains_moment: float32 [2, 960], replicated, may hold values from -128 to 128
- query_square: float32 [960, 960], P('row', 'col'), may hold values from 6553.6 to 26214.4
- key_square: float32 [960, 320], P('row', 'col'), may hold values from 6553.6 to 26214.4
- value_square: float32 [960, 320], P('row', 'col'), may hold values from 6553.6 to 26214.4
- output_square: float32 [960, 960], P('row', 'col'), may hold values from 409.6 to 1638.4
- gate_up_square: float32 [2, 960, 2560], P(None, 'row', 'col'), may hold values from 409.6 to 1638.4
- down_square: float32 [960, 2560], P('row', 'col'), may hold values from 1638.4 to 6553.6
- gains_square: float32 [2, 960], replicated, may hold values from 1638.4 to 6553.6
Outputs:
- block_out: bfloat16 [32768, 960], P(('dp', 'row', 'col'))
- input_grad: bfloat16 [32768, 960], P(('dp', 'row', 'col'))
- query_grad: float32 [960, 960], P('row', 'col')
- query_moment_new: float32 [960, 960], P('row', 'col')
- query_square_new: float32 [960, 960], P('row', 'col')
- query_new: float32 [960, 960], P('row', 'col')
- key_grad: float32 [960, 320], P('row', 'col')
- key_moment_new: float32 [960, 320], P('row', 'col')
- key_square_new: float32 [960, 320], P('row', 'col')
- key_new: float32 [960, 320], P('row', 'col')
- value_grad: float32 [960, 320], P('row', 'col')
- value_moment_new: float32 [960, 320], P('row', 'col')
- value_square_new: float32 [960, 320], P('row', 'col')
- value_new: float32 [960, 320], P('row', 'col')
- output_grad: float32 [960, 960], P('row', 'col')
- output_moment_new: float32 [960, 960], P('row', 'col')
- output_square_new: float32 [960, 960], P('row', 'col')
- output_new: float32 [960, 960], P('row', 'col')
- gate_up_grad: float32 [2, 960, 2560], P(None, 'row', 'col')
- gate_up_moment_new: float32 [2, 960, 2560], P(None, 'row', 'col')
- gate_up_square_new: float32 [2, 960, 2560], P(None, 'row', 'col')
- gate_up_new: float32 [2, 960, 2560], P(None, 'row', 'col')
- down_grad: float32 [960, 2560], P('row', 'col')
- down_moment_new: float32 [960, 2560], P('row', 'col')
- down_square_new: float32 [960, 2560], P('row', 'col')
- down_new: float32 [960, 2560], P('row', 'col')
- gains_grad: float32 [2, 960], replicated
- gains_moment_new: float32 [2, 960], replicated
- gains_square_new: float32 [2, 960], replicated
- gains_new: float32 [2, 960], replicated
The draws below stay inside these ranges and needn't reach their ends.
Inputs may be any that keep to these rules, and one draw needn't show every extreme that they name: `segment_ids`: within each sequence (a run of 1024 consecutive tokens) the segment number starts at 0 and never falls; tokens with one number form one document. `positions`: A token's position rises by one along its segment; a segment that begins inside a sequence begins at 0, while a sequence's first segment may continue a document that began before it.
All inputs are finite; a program needn't handle non-finite values.
Results may differ from the reference program's by a relative error of at most 0.017.
Values may be sent and summed in bfloat16 or wider, within the bound.
A program may use at most 256 MiB of HBM per device.

```python
import math
import jax
import jax.numpy as jnp
from jax import lax

D = 960
HEADS = 15
KV_HEADS = 5
HEAD_DIM = 64
FF = 2560
SEQ = 1024
STEP = 10
KV_WIDTH = 320
TOKENS = 32768


def doc_layout(key):
    seq_count = TOKENS // SEQ
    shortest = SEQ // 5
    length_key, offset_key = jax.random.split(jax.random.fold_in(key, 71))
    doc_lengths = jax.random.randint(length_key, (seq_count, 8), shortest, 2 * SEQ + 1)
    doc_lengths = doc_lengths.at[0, 0].set(2 * SEQ)
    doc_lengths = doc_lengths.at[2].set(jnp.full((8,), shortest, jnp.int32))
    offsets = jax.random.randint(offset_key, (seq_count,), 0, 1 << 30) % doc_lengths[:, 0]
    offsets = offsets.at[0].set(SEQ).at[1].set(0).at[2].set(shortest - 1)
    doc_ends = jnp.cumsum(doc_lengths, axis=1) - offsets[:, None]
    places = jnp.arange(SEQ)
    segments = jnp.sum((doc_ends[:, None, :] <= places[None, :, None]).astype(jnp.int32), axis=-1)
    doc_starts = jnp.concatenate([-offsets[:, None], doc_ends[:, :-1]], axis=1)
    own_start = jnp.take_along_axis(doc_starts, segments, axis=1)
    return (segments.reshape(-1).astype(jnp.int32), (places[None, :] - own_start).reshape(-1).astype(jnp.int32))


def draw_segment_ids(key, part):
    shared = doc_layout(key)
    return shared[0]


def draw_positions(key, part):
    shared = doc_layout(key)
    return shared[1]


def draw_hidden_in(key, part):
    key = jax.random.fold_in(key, 5)
    row_key, col_key, base_key = jax.random.split(key, 3)
    row_scale = jnp.exp(jax.random.uniform(row_key, (TOKENS, 1), jnp.float32, math.log(0.3), math.log(3.0)))
    col_scale = jnp.exp(jax.random.uniform(col_key, (1, D), jnp.float32, math.log(0.3), math.log(3.0)))
    base_values = jnp.clip(jax.random.normal(base_key, (TOKENS, D), jnp.float32), -4.0, 4.0)
    return jnp.clip(base_values * row_scale * col_scale, -30.0, 30.0).astype(jnp.bfloat16)


def shard_levels(key, shape, cuts, low, high):
    def one(position, shards_of):
        heights = jax.random.uniform(jax.random.fold_in(jax.random.fold_in(key, 6), position), (shards_of,), jnp.float32, low / len(cuts), high / len(cuts))
        return jnp.repeat(jnp.exp(heights), shape[position] // shards_of).reshape((-1,) + (1,) * (len(shape) - position - 1))

    factor_of = one(*cuts[0])
    for cut in cuts[1:]:
        factor_of = factor_of * one(*cut)
    return factor_of


def normal_values(key, extent, width, reach, cuts=(), kind=jnp.bfloat16):
    drawn = width * jax.random.normal(key, extent, jnp.float32)
    if cuts:
        drawn = drawn * shard_levels(key, extent, cuts, -0.22, 0.18)
    return jnp.clip(drawn, -reach, reach).astype(kind)


def setup_inputs(seed: int = 0) -> dict:
    keys = jax.random.split(jax.random.key(seed), 26)
    hidden_in = draw_hidden_in(jax.random.fold_in(keys[25], 71), 0)
    cotangent = normal_values(keys[1], (TOKENS, D), 1.0, 6.0, ((0, 32),))
    segment_ids = draw_segment_ids(jax.random.fold_in(keys[25], 71), 0)
    positions = draw_positions(jax.random.fold_in(keys[25], 71), 0)
    query_weight = normal_values(keys[4], (D, D), D ** -0.5, 0.1875, ((0, 2), (1, 4)), jnp.float32)
    key_weight = normal_values(keys[5], (D, KV_WIDTH), D ** -0.5, 0.1875, ((0, 2), (1, 4)), jnp.float32)
    value_weight = normal_values(keys[6], (D, KV_WIDTH), D ** -0.5, 0.1875, ((0, 2), (1, 4)), jnp.float32)
    output_weight = normal_values(keys[7], (D, D), (D // 16) ** -0.5, 0.75, ((0, 2), (1, 4)), jnp.float32)
    gate_up_weight = normal_values(keys[8], (2, D, FF), D ** -0.5, 0.1875, ((1, 2), (2, 4)), jnp.float32)
    down_weight = normal_values(keys[9], (D, FF), FF ** -0.5, 0.125, ((0, 2), (1, 4)), jnp.float32)
    norm_gains = jnp.clip(1.0 + 0.1 * jax.random.normal(keys[10], (2, D), jnp.float32), 0.5, 1.5)
    query_moment = normal_values(keys[11], (D, D), (0.22 * TOKENS ** 0.5), 256.0, ((0, 2), (1, 4)), jnp.float32)
    key_moment = normal_values(keys[12], (D, KV_WIDTH), (0.22 * TOKENS ** 0.5), 256.0, ((0, 2), (1, 4)), jnp.float32)
    value_moment = normal_values(keys[13], (D, KV_WIDTH), (0.22 * TOKENS ** 0.5), 256.0, ((0, 2), (1, 4)), jnp.float32)
    output_moment = normal_values(keys[14], (D, D), (0.055 * TOKENS ** 0.5), 64.0, ((0, 2), (1, 4)), jnp.float32)
    gate_up_moment = normal_values(keys[15], (2, D, FF), (0.055 * TOKENS ** 0.5), 64.0, ((1, 2), (2, 4)), jnp.float32)
    down_moment = normal_values(keys[16], (D, FF), (0.11 * TOKENS ** 0.5), 128.0, ((0, 2), (1, 4)), jnp.float32)
    gains_moment = normal_values(keys[17], (2, D), (0.11 * TOKENS ** 0.5), 128.0, (), jnp.float32)
    query_square = jnp.clip(jnp.exp(math.log(26214.4) - 1.3862944 * jax.random.uniform(keys[18], (D, D), jnp.float32) ** shard_levels(keys[18], (D, D), ((0, 2), (1, 4)), -0.2, 0.2)), 6553.6, 26214.4)
    key_square = jnp.clip(jnp.exp(math.log(26214.4) - 1.3862944 * jax.random.uniform(keys[19], (D, KV_WIDTH), jnp.float32) ** shard_levels(keys[19], (D, KV_WIDTH), ((0, 2), (1, 4)), -0.2, 0.2)), 6553.6, 26214.4)
    value_square = jnp.clip(jnp.exp(math.log(26214.4) - 1.3862944 * jax.random.uniform(keys[20], (D, KV_WIDTH), jnp.float32) ** shard_levels(keys[20], (D, KV_WIDTH), ((0, 2), (1, 4)), -0.2, 0.2)), 6553.6, 26214.4)
    output_square = jnp.clip(jnp.exp(math.log(1638.4) - 1.3862944 * jax.random.uniform(keys[21], (D, D), jnp.float32) ** shard_levels(keys[21], (D, D), ((0, 2), (1, 4)), -0.2, 0.2)), 409.6, 1638.4)
    gate_up_square = jnp.clip(jnp.exp(math.log(1638.4) - 1.3862944 * jax.random.uniform(keys[22], (2, D, FF), jnp.float32) ** shard_levels(keys[22], (2, D, FF), ((1, 2), (2, 4)), -0.2, 0.2)), 409.6, 1638.4)
    down_square = jnp.clip(jnp.exp(math.log(6553.6) - 1.3862944 * jax.random.uniform(keys[23], (D, FF), jnp.float32) ** shard_levels(keys[23], (D, FF), ((0, 2), (1, 4)), -0.2, 0.2)), 1638.4, 6553.6)
    gains_square = jnp.clip(jnp.exp(jax.random.uniform(keys[24], (2, D), jnp.float32, math.log(1638.4), math.log(6553.6))), 1638.4, 6553.6)
    return {"hidden_in": hidden_in, "cotangent": cotangent, "segment_ids": segment_ids, "positions": positions, "query_weight": query_weight, "key_weight": key_weight, "value_weight": value_weight, "output_weight": output_weight, "gate_up_weight": gate_up_weight, "down_weight": down_weight, "norm_gains": norm_gains, "query_moment": query_moment, "key_moment": key_moment, "value_moment": value_moment, "output_moment": output_moment, "gate_up_moment": gate_up_moment, "down_moment": down_moment, "gains_moment": gains_moment, "query_square": query_square, "key_square": key_square, "value_square": value_square, "output_square": output_square, "gate_up_square": gate_up_square, "down_square": down_square, "gains_square": gains_square}


@jax.custom_vjp
def low(v):
    return lax.optimization_barrier(v.astype(jnp.bfloat16)).astype(jnp.float32)

@jax.custom_vjp
def low_back(v):
    return v

def low_keep(v):
    return (low(v), None)

def low_pass(kept, grad):
    return (grad,)

def back_keep(v):
    return (v, None)

def back_low(kept, grad):
    return (low(grad),)
low.defvjp(low_keep, low_pass)
low_back.defvjp(back_keep, back_low)
norm_eps = 1e-05
rope_base = 100000.0
beta_one = 0.9
beta_two = 0.95
adam_eps = 1e-08
decay_rate = 0.1
matrix_rate = 0.1
gain_rate = 1.0
masked_fill = -1000000000.0
highest = lax.Precision.HIGHEST

def norm_rows(values, scales):
    inverse = lax.rsqrt(lax.optimization_barrier(jnp.mean(values * values, axis=-1, keepdims=True)) + norm_eps)
    return values * inverse * scales

def rope_tables(positions):
    ladder = jnp.arange(HEAD_DIM // 2, dtype=jnp.float32) * (2.0 / HEAD_DIM)
    frequency = jnp.exp(ladder * -math.log(rope_base))
    angles = positions.astype(jnp.float32)[:, None] * frequency[None, :]
    return (jnp.cos(angles), jnp.sin(angles))

def rotate(values, cos_table, sine_table):
    half_dim = HEAD_DIM // 2
    first_half = values[..., :half_dim]
    second_half = values[..., half_dim:]
    cos_rows = cos_table[:, None, :]
    sin_rows = sine_table[:, None, :]
    return jnp.concatenate([first_half * cos_rows - second_half * sin_rows, second_half * cos_rows + first_half * sin_rows], axis=-1)

def attend(packed):
    queries, key_rows, values, segments = packed
    group_size = HEADS // KV_HEADS
    places = jnp.arange(SEQ)
    allowed = (places[:, None] >= places[None, :]) & (segments[:, None] == segments[None, :])
    grouped = queries.reshape(SEQ, KV_HEADS, group_size, HEAD_DIM)
    scores = jnp.einsum('qkgd,skd->kgqs', grouped, key_rows, precision=highest) * HEAD_DIM ** (-0.5)
    scores = jnp.where(allowed[None, None], low_back(scores), masked_fill)
    summit = lax.optimization_barrier(jnp.max(scores, axis=-1, keepdims=True))
    powers = jnp.exp(scores - summit)
    softmaxed = low(powers / lax.optimization_barrier(jnp.sum(powers, axis=-1, keepdims=True)))
    blended = jnp.einsum('kgqs,skd->qkgd', softmaxed, values, precision=highest)
    return blended.reshape(SEQ, HEADS * HEAD_DIM)

def layer_group(weights, inputs, segments, positions):
    query_low, key_low, value_low, output_low, gate_up_low, down_low, norm_scales = weights
    count_rows = inputs.shape[0]
    seq_count = count_rows // SEQ
    normed_one = low(norm_rows(inputs, norm_scales[0]))
    query_pre = low_back(jnp.dot(normed_one, query_low, precision=highest))
    key_pre = low_back(jnp.dot(normed_one, key_low, precision=highest))
    value_rows = low(low_back(jnp.dot(normed_one, value_low, precision=highest)))
    cos_table, sine_table = rope_tables(positions)
    queries = low(rotate(query_pre.reshape(count_rows, HEADS, HEAD_DIM), cos_table, sine_table))
    key_rows = low(rotate(key_pre.reshape(count_rows, KV_HEADS, HEAD_DIM), cos_table, sine_table))
    blended = lax.map(jax.checkpoint(attend), (queries.reshape(seq_count, SEQ, HEADS, HEAD_DIM), key_rows.reshape(seq_count, SEQ, KV_HEADS, HEAD_DIM), value_rows.reshape(seq_count, SEQ, KV_HEADS, HEAD_DIM), segments.reshape(seq_count, SEQ)))
    heads_out = low(low_back(blended.reshape(count_rows, HEADS * HEAD_DIM)))
    middle = inputs + low_back(jnp.dot(heads_out, output_low, precision=highest))
    normed_two = low(norm_rows(middle, norm_scales[1]))
    gate_pre = low_back(jnp.dot(normed_two, gate_up_low[0], precision=highest))
    up_pre = low_back(jnp.dot(normed_two, gate_up_low[1], precision=highest))
    hidden = low(gate_pre / (1.0 + jnp.exp(-gate_pre)) * up_pre)
    return middle + jnp.dot(hidden, down_low.T, precision=highest)

def forward(inputs, segments, positions, params):
    query_weight, key_weight, value_weight, output_weight, gate_up_weight, down_weight, norm_gains = params
    weights = (low(query_weight), low(key_weight), low(value_weight), low(output_weight), low(gate_up_weight), low(down_weight), norm_gains)
    span_rows = 4 * SEQ
    group_count = inputs.shape[0] // span_rows

    def one_group(packed):
        return layer_group(weights, packed[0], packed[1], packed[2])
    outputs = lax.map(jax.checkpoint(one_group), (inputs.reshape(group_count, span_rows, D), segments.reshape(group_count, span_rows), positions.reshape(group_count, span_rows)))
    return outputs.reshape(group_count * span_rows, D)

def adam_step(weight, gradient, moment, square, step_rate, decay_factor):
    moment_new = beta_one * moment + (1.0 - beta_one) * gradient
    square_new = beta_two * square + (1.0 - beta_two) * gradient * gradient
    scaled_step = moment_new / (1.0 - beta_one ** STEP) / (jnp.sqrt(square_new / (1.0 - beta_two ** STEP)) + adam_eps)
    return (moment_new, square_new, weight - step_rate * (scaled_step + decay_factor * weight))

def reference(hidden_in, cotangent, segment_ids, positions, query_weight, key_weight, value_weight, output_weight, gate_up_weight, down_weight, norm_gains, query_moment, key_moment, value_moment, output_moment, gate_up_moment, down_moment, gains_moment, query_square, key_square, value_square, output_square, gate_up_square, down_square, gains_square):
    inputs = hidden_in.astype(jnp.float32)
    params = (query_weight, key_weight, value_weight, output_weight, gate_up_weight, down_weight, norm_gains)

    def layer_call(rows_in, *weights):
        return forward(rows_in, segment_ids, positions, weights)
    outputs, pullback = jax.vjp(layer_call, inputs, *params)
    gradients = pullback(cotangent.astype(jnp.float32))
    query_grad = gradients[1]
    key_grad = gradients[2]
    value_grad = gradients[3]
    output_grad = gradients[4]
    gate_up_grad = gradients[5]
    down_grad = gradients[6]
    gains_grad = gradients[7]
    query_moment_new, query_square_new, query_new = adam_step(query_weight, query_grad, query_moment, query_square, matrix_rate, decay_rate)
    key_moment_new, key_square_new, key_new = adam_step(key_weight, key_grad, key_moment, key_square, matrix_rate, decay_rate)
    value_moment_new, value_square_new, value_new = adam_step(value_weight, value_grad, value_moment, value_square, matrix_rate, decay_rate)
    output_moment_new, output_square_new, output_new = adam_step(output_weight, output_grad, output_moment, output_square, matrix_rate, decay_rate)
    gate_up_moment_new, gate_up_square_new, gate_up_new = adam_step(gate_up_weight, gate_up_grad, gate_up_moment, gate_up_square, matrix_rate, decay_rate)
    down_moment_new, down_square_new, down_new = adam_step(down_weight, down_grad, down_moment, down_square, matrix_rate, decay_rate)
    gains_moment_new, gains_square_new, gains_new = adam_step(norm_gains, gains_grad, gains_moment, gains_square, gain_rate, 0.0)
    return (outputs.astype(jnp.bfloat16), gradients[0].astype(jnp.bfloat16), query_grad, query_moment_new, query_square_new, query_new, key_grad, key_moment_new, key_square_new, key_new, value_grad, value_moment_new, value_square_new, value_new, output_grad, output_moment_new, output_square_new, output_new, gate_up_grad, gate_up_moment_new, gate_up_square_new, gate_up_new, down_grad, down_moment_new, down_square_new, down_new, gains_grad, gains_moment_new, gains_square_new, gains_new)
```

```python
import math

import jax
import jax.numpy as jnp
from jax import lax
from jax.experimental import pallas as pl
from jax.experimental.pallas import tpu as pltpu
from jax.sharding import PartitionSpec as P

HEADS = 15
KV_HEADS = 5
HEAD_DIM = 64
SEQ = 1024
STEP = 10
GROUP = HEADS // KV_HEADS
TILE = 256


norm_eps = 1e-05
rope_base = 100000.0
beta_one = 0.9
beta_two = 0.95
adam_eps = 1e-08
decay_rate = 0.1
matrix_rate = 0.1
gain_rate = 1.0
masked_fill = -1000000000.0


def rope_tables(positions):
    ladder = jnp.arange(HEAD_DIM // 2, dtype=jnp.float32) * (2.0 / HEAD_DIM)
    frequency = jnp.exp(ladder * -math.log(rope_base))
    angles = frequency[:, None] * positions.astype(jnp.float32)[None, :]
    return (jnp.cos(angles), jnp.sin(angles))


def rotate(values, cos_table, sine_table):
    half_dim = HEAD_DIM // 2
    upper = values[:half_dim]
    lower = values[half_dim:]
    return jnp.concatenate(
        [upper * cos_table - lower * sine_table, lower * cos_table + upper * sine_table], axis=0
    )


def dot(left, right, dims=((1,), (0,))):
    return lax.dot_general(left, right, (dims, ((), ())), preferred_element_type=jnp.float32)


def fill_bias(bias, seg_row, seg_col):
    @pl.when(pl.program_id(0) == 0)
    def _():
        for start in range(0, SEQ, TILE):
            size = start + TILE
            earlier = lax.broadcasted_iota(jnp.int32, (size, TILE), 0)
            later = lax.broadcasted_iota(jnp.int32, (size, TILE), 1) + start
            same = seg_col[:size] == seg_row[:, start:size]
            bias[:size, start:size] = jnp.where((earlier <= later) & same, 0.0, masked_fill)


def attend_kernel(
    q_ref, k_ref, v_ref, cos_ref, sin_ref, seg_row, seg_col, low_ref, out_ref, log_ref, bias
):
    fill_bias(bias, seg_row, seg_col)
    pair = pl.program_id(0)
    cos_table = cos_ref[...]
    sine_table = sin_ref[...]
    keys = rotate(k_ref[...], cos_table, sine_table).astype(jnp.bfloat16)
    values = v_ref[...].astype(jnp.bfloat16)
    query_width = HEADS * HEAD_DIM
    kv_width = KV_HEADS * HEAD_DIM
    place = pl.multiple_of(pair * HEAD_DIM, HEAD_DIM)
    low_ref[pl.ds(query_width + place, HEAD_DIM), :] = keys
    low_ref[pl.ds(query_width + kv_width + place, HEAD_DIM), :] = values
    key_rows = keys.T
    for head in range(GROUP):
        rows = slice(head * HEAD_DIM, (head + 1) * HEAD_DIM)
        queries = rotate(q_ref[rows, :], cos_table, sine_table).astype(jnp.bfloat16)
        low_ref[pl.ds(pl.multiple_of((pair * GROUP + head) * HEAD_DIM, HEAD_DIM), HEAD_DIM), :] = (
            queries
        )
        scaled = queries * HEAD_DIM ** (-0.5)
        for start in range(0, SEQ, TILE):
            size = start + TILE
            scores = dot(key_rows[:size], scaled[:, start:size]) + bias[:size, start:size]
            summit = jnp.max(scores, axis=0, keepdims=True)
            powers = jnp.exp(scores - summit)
            totals = jnp.sum(powers, axis=0, keepdims=True)
            blended = dot(values[:, :size], powers.astype(jnp.bfloat16)) / totals
            out_ref[rows, start:size] = blended.astype(jnp.bfloat16)
            log_ref[0, head : head + 1, start:size] = summit + jnp.log(totals)


def attend_back_kernel(
    q_ref,
    k_ref,
    v_ref,
    grad_ref,
    log_ref,
    cos_ref,
    sin_ref,
    seg_row,
    seg_col,
    out_ref,
    bias,
    key_total,
    value_total,
):
    fill_bias(bias, seg_row, seg_col)
    pair = pl.program_id(0)
    cos_table = cos_ref[...]
    sine_table = -sin_ref[...]
    scale = HEAD_DIM ** (-0.5)
    keys = k_ref[...]
    key_rows = keys.T
    value_rows = v_ref[...].T
    key_total[...] = jnp.zeros_like(key_total)
    value_total[...] = jnp.zeros_like(value_total)
    for head in range(GROUP):
        rows = slice(head * HEAD_DIM, (head + 1) * HEAD_DIM)
        queries = q_ref[rows, :]
        scaled = queries * scale
        query_rows = scaled.T
        incoming = grad_ref[rows, :]
        incoming_rows = incoming.T
        parts = []
        for start in range(0, SEQ, TILE):
            size = start + TILE
            scores = dot(key_rows[:size], scaled[:, start:size]) + bias[:size, start:size]
            chances = jnp.exp(scores - log_ref[0, head : head + 1, start:size])
            chance_grad = dot(value_rows[:size], incoming[:, start:size])
            centre = jnp.sum(chances * chance_grad, axis=0, keepdims=True)
            score_grad = (chances * (chance_grad - centre)).astype(jnp.bfloat16)
            parts.append(dot(keys[:, :size], score_grad) * scale)
            key_total[:size] += dot(score_grad, query_rows[start:size])
            value_total[:size] += dot(chances.astype(jnp.bfloat16), incoming_rows[start:size])
        query_grad = rotate(jnp.concatenate(parts, axis=1), cos_table, sine_table)
        out_ref[pl.ds(pl.multiple_of((pair * GROUP + head) * HEAD_DIM, HEAD_DIM), HEAD_DIM), :] = (
            query_grad.astype(jnp.bfloat16)
        )
    query_width = HEADS * HEAD_DIM
    kv_width = KV_HEADS * HEAD_DIM
    place = pl.multiple_of(pair * HEAD_DIM, HEAD_DIM)
    key_grad = rotate(key_total[...].T, cos_table, sine_table)
    out_ref[pl.ds(query_width + place, HEAD_DIM), :] = key_grad.astype(jnp.bfloat16)
    out_ref[pl.ds(query_width + kv_width + place, HEAD_DIM), :] = (
        value_total[...].T.astype(jnp.bfloat16)
    )


def whole_spec(*shape):
    return pl.BlockSpec(shape, lambda step: (0,) * len(shape))


def head_specs():
    return [
        pl.BlockSpec((GROUP * HEAD_DIM, SEQ), lambda j: (j, 0)),
        pl.BlockSpec((HEAD_DIM, SEQ), lambda j: (HEADS + j, 0)),
        pl.BlockSpec((HEAD_DIM, SEQ), lambda j: (HEADS + KV_HEADS + j, 0)),
    ]


def attend(projected, cos_table, sine_table, segments):
    half_dim = HEAD_DIM // 2
    width = projected.shape[0]
    return pl.pallas_call(
        attend_kernel,
        grid=(KV_HEADS,),
        in_specs=head_specs()
        + [
            whole_spec(half_dim, SEQ),
            whole_spec(half_dim, SEQ),
            whole_spec(1, SEQ),
            whole_spec(SEQ, 1),
        ],
        out_specs=[
            whole_spec(width, SEQ),
            pl.BlockSpec((GROUP * HEAD_DIM, SEQ), lambda j: (j, 0)),
            pl.BlockSpec((1, GROUP, SEQ), lambda j: (j, 0, 0)),
        ],
        out_shape=[
            jax.ShapeDtypeStruct((width, SEQ), jnp.bfloat16),
            jax.ShapeDtypeStruct((HEADS * HEAD_DIM, SEQ), jnp.bfloat16),
            jax.ShapeDtypeStruct((KV_HEADS, GROUP, SEQ), jnp.float32),
        ],
        scratch_shapes=[pltpu.VMEM((SEQ, SEQ), jnp.float32)],
        compiler_params=pltpu.CompilerParams(vmem_limit_bytes=48 << 20),
        cost_estimate=pl.CostEstimate(
            flops=20 * SEQ * SEQ * HEADS * HEAD_DIM,
            bytes_accessed=16 << 20,
            transcendentals=HEADS * SEQ * SEQ,
        ),
        name="attend",
    )(
        projected,
        projected,
        projected,
        cos_table,
        sine_table,
        segments.reshape(1, SEQ),
        segments.reshape(SEQ, 1),
    )


def attend_back(low, blended_grad, log_totals, cos_table, sine_table, segments):
    half_dim = HEAD_DIM // 2
    width = low.shape[0]
    return pl.pallas_call(
        attend_back_kernel,
        grid=(KV_HEADS,),
        in_specs=head_specs()
        + [
            pl.BlockSpec((GROUP * HEAD_DIM, SEQ), lambda j: (j, 0)),
            pl.BlockSpec((1, GROUP, SEQ), lambda j: (j, 0, 0)),
            whole_spec(half_dim, SEQ),
            whole_spec(half_dim, SEQ),
            whole_spec(1, SEQ),
            whole_spec(SEQ, 1),
        ],
        out_specs=whole_spec(width, SEQ),
        out_shape=jax.ShapeDtypeStruct((width, SEQ), jnp.bfloat16),
        scratch_shapes=[
            pltpu.VMEM((SEQ, SEQ), jnp.float32),
            pltpu.VMEM((SEQ, HEAD_DIM), jnp.float32),
            pltpu.VMEM((SEQ, HEAD_DIM), jnp.float32),
        ],
        compiler_params=pltpu.CompilerParams(vmem_limit_bytes=48 << 20),
        cost_estimate=pl.CostEstimate(
            flops=60 * SEQ * SEQ * HEADS * HEAD_DIM,
            bytes_accessed=16 << 20,
            transcendentals=HEADS * SEQ * SEQ,
        ),
        name="attend_back",
    )(
        low,
        low,
        low,
        blended_grad,
        log_totals,
        cos_table,
        sine_table,
        segments.reshape(1, SEQ),
        segments.reshape(SEQ, 1),
    )


def mlp_kernel(
    normed_ref,
    normed_turned,
    back_ref,
    back_turned,
    pair_ref,
    down_ref,
    out_ref,
    grad_ref,
    pair_out,
    down_out,
    hidden_keep,
    gate_keep,
    up_keep,
):
    first = pl.program_id(0) == 0
    height = pair_ref.shape[0] * pair_ref.shape[3]
    width = pair_ref.shape[4]
    token_count = normed_ref.shape[0]

    @pl.when(first)
    def _():
        out_ref[...] = jnp.zeros_like(out_ref)
        grad_ref[...] = jnp.zeros_like(grad_ref)

    gate_weight = pair_ref[:, 0, 0].reshape(height, width)
    up_weight = pair_ref[:, 0, 1].reshape(height, width)
    down_weight = down_ref[:, 0].reshape(height, width)

    def forward(step, carry):
        rows = pl.ds(pl.multiple_of(step * TILE, TILE), TILE)
        normed = normed_ref[rows, :]
        gate_pre = dot(normed, gate_weight)
        up_pre = dot(normed, up_weight)
        hidden_grad = dot(back_ref[rows, :], down_weight)
        sigmoid_gate = 1.0 / (1.0 + jnp.exp(-gate_pre))
        silu_gate = gate_pre * sigmoid_gate
        hidden = (silu_gate * up_pre).astype(jnp.bfloat16)
        gate_grad = (
            hidden_grad * up_pre * sigmoid_gate * (1.0 + gate_pre * (1.0 - sigmoid_gate))
        ).astype(jnp.bfloat16)
        up_grad = (hidden_grad * silu_gate).astype(jnp.bfloat16)
        hidden_keep[rows, :] = hidden
        gate_keep[rows, :] = gate_grad
        up_keep[rows, :] = up_grad
        out_ref[rows, :] += dot(hidden, down_weight, ((1,), (1,)))
        grad_ref[rows, :] += dot(gate_grad, gate_weight, ((1,), (1,))) + dot(
            up_grad, up_weight, ((1,), (1,))
        )
        return carry

    lax.fori_loop(0, token_count // TILE, forward, 0)
    block_rows = pair_ref.shape[3]
    for block in range(pair_ref.shape[0]):
        rows = slice(block * block_rows, (block + 1) * block_rows)
        left = normed_turned[rows, :]
        pair_out[block, 0, 0] = dot(left, gate_keep[...]).astype(jnp.bfloat16)
        pair_out[block, 0, 1] = dot(left, up_keep[...]).astype(jnp.bfloat16)
        down_out[block, 0] = dot(back_turned[rows, :], hidden_keep[...]).astype(jnp.bfloat16)


def mlp(normed, back, pair_grid, down_grid):
    token_count, features = normed.shape
    row_count, col_count, _, height, width = pair_grid.shape
    aligned = height % 16 == 0 and width % 128 == 0
    if not aligned:
        units = col_count * width
        pieces = units // 640
        pair_grid = pair_grid.transpose(2, 0, 3, 1, 4).reshape(1, 2, features, pieces, 640)
        pair_grid = pair_grid.transpose(0, 3, 1, 2, 4)
        down_grid = down_grid.transpose(0, 2, 1, 3).reshape(1, features, pieces, 640)
        down_grid = down_grid.transpose(0, 2, 1, 3)
    rows, cols, _, tall, wide = pair_grid.shape
    single = pl.Buffered(1)

    def fixed(*shape):
        return pl.BlockSpec(shape, lambda c: (0, 0), pipeline_mode=single)

    pair_spec = pl.BlockSpec((rows, 1, 2, tall, wide), lambda c: (0, c, 0, 0, 0))
    down_spec = pl.BlockSpec((rows, 1, tall, wide), lambda c: (0, c, 0, 0))
    outs = pl.pallas_call(
        mlp_kernel,
        grid=(cols,),
        in_specs=[
            fixed(token_count, features),
            fixed(features, token_count),
            fixed(token_count, features),
            fixed(features, token_count),
            pair_spec,
            down_spec,
        ],
        out_specs=[
            fixed(token_count, features),
            fixed(token_count, features),
            pair_spec,
            down_spec,
        ],
        out_shape=[
            jax.ShapeDtypeStruct((token_count, features), jnp.float32),
            jax.ShapeDtypeStruct((token_count, features), jnp.float32),
            jax.ShapeDtypeStruct(pair_grid.shape, jnp.bfloat16),
            jax.ShapeDtypeStruct(down_grid.shape, jnp.bfloat16),
        ],
        scratch_shapes=[pltpu.VMEM((token_count, wide), jnp.bfloat16)] * 3,
        compiler_params=pltpu.CompilerParams(vmem_limit_bytes=58 << 20),
        cost_estimate=pl.CostEstimate(
            flops=18 * token_count * features * cols * wide,
            bytes_accessed=64 << 20,
            transcendentals=token_count * cols * wide,
        ),
        name="mlp",
    )(normed, normed.T, back, back.T, pair_grid, down_grid)
    mlp_out, normed_grad, pair_grad, down_grad = outs
    if not aligned:
        pair_grad = pair_grad.transpose(0, 2, 3, 1, 4).reshape(
            2, row_count, height, col_count, width
        )
        pair_grad = pair_grad.transpose(1, 3, 0, 2, 4)
        down_grad = down_grad.transpose(0, 2, 1, 3).reshape(row_count, height, col_count, width)
        down_grad = down_grad.transpose(0, 2, 1, 3)
    return mlp_out, normed_grad, pair_grad, down_grad


def from_grid(stack, row_count, col_count):
    _, height, width = stack.shape
    shaped = stack.reshape(row_count, col_count, height, width).transpose(0, 2, 1, 3)
    return shaped.reshape(row_count * height, col_count * width)


def into_grid(whole, row_count, col_count):
    height = whole.shape[0] // row_count
    width = whole.shape[1] // col_count
    shaped = whole.reshape(row_count, height, col_count, width).transpose(0, 2, 1, 3)
    return shaped.reshape(row_count * col_count, height, width)


def norm_backward(inputs, inverse, scales, incoming):
    weighted = incoming * scales
    gain_part = jnp.sum(incoming * inputs * inverse, axis=0)
    input_part = inverse * weighted - inputs * inverse**3 * jnp.mean(
        weighted * inputs, axis=-1, keepdims=True
    )
    return (gain_part, input_part)


def adam_step(weight, gradient, moment, square, step_rate, decay_factor):
    moment_new = beta_one * moment + (1.0 - beta_one) * gradient
    square_new = beta_two * square + (1.0 - beta_two) * gradient * gradient
    scaled_step = (
        moment_new
        / (1.0 - beta_one**STEP)
        / (jnp.sqrt(square_new / (1.0 - beta_two**STEP)) + adam_eps)
    )
    return (moment_new, square_new, weight - step_rate * (scaled_step + decay_factor * weight))


def shards(
    hidden_in,
    cotangent,
    segment_ids,
    positions,
    query_weight,
    key_weight,
    value_weight,
    output_weight,
    gate_up_weight,
    down_weight,
    norm_gains,
    query_moment,
    key_moment,
    value_moment,
    output_moment,
    gate_up_moment,
    down_moment,
    gains_moment,
    query_square,
    key_square,
    value_square,
    output_square,
    gate_up_square,
    down_square,
    gains_square,
):
    row_count = lax.axis_size("row")
    col_count = lax.axis_size("col")
    query_part = query_weight.shape[1]
    key_part = key_weight.shape[1]
    cuts = (query_part, query_part + key_part, query_part + 2 * key_part)
    query_width = HEADS * HEAD_DIM
    kv_width = KV_HEADS * HEAD_DIM

    def gather(block):
        return lax.all_gather(block[None], ("row", "col"), axis=0, tiled=True)

    def scatter(stack):
        return lax.psum_scatter(stack, ("row", "col"), scatter_dimension=0, tiled=True)[0]

    def total(part):
        return lax.psum(part, "dp").astype(jnp.float32)

    first_stack = gather(
        jnp.concatenate([query_weight, key_weight, value_weight, output_weight], axis=1).astype(
            jnp.bfloat16
        )
    )
    gate_up_stack = gather(gate_up_weight.astype(jnp.bfloat16))
    down_stack = gather(down_weight.astype(jnp.bfloat16))
    first_low = jnp.concatenate(
        [
            from_grid(first_stack[:, :, : cuts[0]], row_count, col_count),
            from_grid(first_stack[:, :, cuts[0] : cuts[1]], row_count, col_count),
            from_grid(first_stack[:, :, cuts[1] : cuts[2]], row_count, col_count),
        ],
        axis=1,
    )
    output_low = from_grid(first_stack[:, :, cuts[2] :], row_count, col_count)
    gate_up_grid = gate_up_stack.reshape((row_count, col_count) + gate_up_weight.shape)
    down_grid = down_stack.reshape((row_count, col_count) + down_weight.shape)

    cos_table, sine_table = rope_tables(positions)
    inputs = hidden_in.astype(jnp.float32)
    inverse_one = lax.rsqrt(jnp.mean(inputs * inputs, axis=-1, keepdims=True) + norm_eps)
    normed_one = (inputs * inverse_one * norm_gains[0]).astype(jnp.bfloat16)
    projected = dot(first_low, normed_one, ((0,), (1,)))
    low, blended, log_totals = attend(projected, cos_table, sine_table, segment_ids)
    middle = inputs + dot(blended, output_low, ((0,), (0,)))
    inverse_two = lax.rsqrt(jnp.mean(middle * middle, axis=-1, keepdims=True) + norm_eps)
    normed_two = (middle * inverse_two * norm_gains[1]).astype(jnp.bfloat16)
    mlp_out, normed_two_grad, gate_up_block, down_block = mlp(
        normed_two, cotangent, gate_up_grid, down_grid
    )
    gate_up_part = scatter(gate_up_block.reshape(gate_up_stack.shape))
    down_part = scatter(down_block.reshape(down_stack.shape))
    block_out = (middle + mlp_out).astype(jnp.bfloat16)
    gain_two, middle_part = norm_backward(middle, inverse_two, norm_gains[1], normed_two_grad)
    middle_grad = cotangent.astype(jnp.float32) + middle_part
    middle_low = middle_grad.astype(jnp.bfloat16)
    output_block = dot(blended, middle_low, ((1,), (0,))).astype(jnp.bfloat16)
    output_part = scatter(into_grid(output_block, row_count, col_count))
    blended_grad = dot(output_low, middle_low, ((1,), (1,))).astype(jnp.bfloat16)
    projected_grad = attend_back(
        low, blended_grad, log_totals, cos_table, sine_table, segment_ids
    )
    projected_grad, gate_up_part, down_part, output_part = lax.optimization_barrier(
        (projected_grad, gate_up_part, down_part, output_part)
    )
    gate_up_sum = total(gate_up_part)
    down_sum = total(down_part)
    output_sum = total(output_part)
    first_block = dot(normed_one, projected_grad, ((0,), (1,))).astype(jnp.bfloat16)
    first_part = scatter(
        jnp.concatenate(
            [
                into_grid(first_block[:, :query_width], row_count, col_count),
                into_grid(
                    first_block[:, query_width : query_width + kv_width], row_count, col_count
                ),
                into_grid(first_block[:, query_width + kv_width :], row_count, col_count),
            ],
            axis=2,
        )
    )
    first_part, gate_up_sum, down_sum, output_sum = lax.optimization_barrier(
        (first_part, gate_up_sum, down_sum, output_sum)
    )
    first_sum = total(first_part)
    normed_one_grad = dot(projected_grad, first_low, ((0,), (1,)))
    gain_one, input_part = norm_backward(inputs, inverse_one, norm_gains[0], normed_one_grad)
    input_grad = (middle_grad + input_part).astype(jnp.bfloat16)
    reduced = (
        first_sum[:, : cuts[0]],
        first_sum[:, cuts[0] : cuts[1]],
        first_sum[:, cuts[1] :],
        output_sum,
        gate_up_sum,
        down_sum,
    )
    gains_grad = lax.psum(jnp.stack([gain_one, gain_two]), ("dp", "row", "col"))
    query_update = adam_step(
        query_weight, reduced[0], query_moment, query_square, matrix_rate, decay_rate
    )
    key_update = adam_step(key_weight, reduced[1], key_moment, key_square, matrix_rate, decay_rate)
    value_update = adam_step(
        value_weight, reduced[2], value_moment, value_square, matrix_rate, decay_rate
    )
    output_update = adam_step(
        output_weight, reduced[3], output_moment, output_square, matrix_rate, decay_rate
    )
    gate_up_update = adam_step(
        gate_up_weight, reduced[4], gate_up_moment, gate_up_square, matrix_rate, decay_rate
    )
    down_update = adam_step(
        down_weight, reduced[5], down_moment, down_square, matrix_rate, decay_rate
    )
    gains_update = adam_step(norm_gains, gains_grad, gains_moment, gains_square, gain_rate, 0.0)
    return (
        block_out,
        input_grad,
        reduced[0],
        query_update[0],
        query_update[1],
        query_update[2],
        reduced[1],
        key_update[0],
        key_update[1],
        key_update[2],
        reduced[2],
        value_update[0],
        value_update[1],
        value_update[2],
        reduced[3],
        output_update[0],
        output_update[1],
        output_update[2],
        reduced[4],
        gate_up_update[0],
        gate_up_update[1],
        gate_up_update[2],
        reduced[5],
        down_update[0],
        down_update[1],
        down_update[2],
        gains_grad,
        gains_update[0],
        gains_update[1],
        gains_update[2],
    )


def solution(mesh):
    in_specs = (
        P(("dp", "row", "col"), None),
        P(("dp", "row", "col"), None),
        P(("dp", "row", "col")),
        P(("dp", "row", "col")),
        P("row", "col"),
        P("row", "col"),
        P("row", "col"),
        P("row", "col"),
        P(None, "row", "col"),
        P("row", "col"),
        P(),
        P("row", "col"),
        P("row", "col"),
        P("row", "col"),
        P("row", "col"),
        P(None, "row", "col"),
        P("row", "col"),
        P(),
        P("row", "col"),
        P("row", "col"),
        P("row", "col"),
        P("row", "col"),
        P(None, "row", "col"),
        P("row", "col"),
        P(),
    )
    out_specs = (
        P(("dp", "row", "col"), None),
        P(("dp", "row", "col"), None),
        P("row", "col"),
        P("row", "col"),
        P("row", "col"),
        P("row", "col"),
        P("row", "col"),
        P("row", "col"),
        P("row", "col"),
        P("row", "col"),
        P("row", "col"),
        P("row", "col"),
        P("row", "col"),
        P("row", "col"),
        P("row", "col"),
        P("row", "col"),
        P("row", "col"),
        P("row", "col"),
        P(None, "row", "col"),
        P(None, "row", "col"),
        P(None, "row", "col"),
        P(None, "row", "col"),
        P("row", "col"),
        P("row", "col"),
        P("row", "col"),
        P("row", "col"),
        P(),
        P(),
        P(),
        P(),
    )
    return jax.shard_map(shards, mesh=mesh, in_specs=in_specs, out_specs=out_specs, check_vma=False)
```

```python
import math

import jax
import jax.numpy as jnp
from jax import lax
from jax.experimental import pallas as pl
from jax.experimental.pallas import tpu as pltpu
from jax.sharding import PartitionSpec as P

HEADS = 15
KV_HEADS = 5
HEAD_DIM = 64
SEQ = 1024
STEP = 10
GROUP = HEADS // KV_HEADS
TILE = 256


norm_eps = 1e-05
rope_base = 100000.0
beta_one = 0.9
beta_two = 0.95
adam_eps = 1e-08
decay_rate = 0.1
matrix_rate = 0.1
gain_rate = 1.0
masked_fill = -1000000000.0


def rope_tables(positions):
    ladder = jnp.arange(HEAD_DIM // 2, dtype=jnp.float32) * (2.0 / HEAD_DIM)
    frequency = jnp.exp(ladder * -math.log(rope_base))
    angles = frequency[:, None] * positions.astype(jnp.float32)[None, :]
    return (jnp.cos(angles), jnp.sin(angles))


def rotate(values, cos_table, sine_table):
    half_dim = HEAD_DIM // 2
    upper = values[:half_dim]
    lower = values[half_dim:]
    return jnp.concatenate(
        [upper * cos_table - lower * sine_table, lower * cos_table + upper * sine_table], axis=0
    )


def dot(left, right, dims=((1,), (0,))):
    return lax.dot_general(left, right, (dims, ((), ())), preferred_element_type=jnp.float32)


def fill_bias(bias, seg_row, seg_col):
    @pl.when(pl.program_id(0) == 0)
    def _():
        for start in range(0, SEQ, TILE):
            size = start + TILE
            earlier = lax.broadcasted_iota(jnp.int32, (size, TILE), 0)
            later = lax.broadcasted_iota(jnp.int32, (size, TILE), 1) + start
            same = seg_col[:size] == seg_row[:, start:size]
            bias[:size, start:size] = jnp.where((earlier <= later) & same, 0.0, masked_fill)


def attend_kernel(
    q_ref, k_ref, v_ref, cos_ref, sin_ref, seg_row, seg_col, low_ref, out_ref, log_ref, bias
):
    fill_bias(bias, seg_row, seg_col)
    pair = pl.program_id(0)
    cos_table = cos_ref[...]
    sine_table = sin_ref[...]
    keys = rotate(k_ref[...], cos_table, sine_table).astype(jnp.bfloat16)
    values = v_ref[...].astype(jnp.bfloat16)
    query_width = HEADS * HEAD_DIM
    kv_width = KV_HEADS * HEAD_DIM
    place = pl.multiple_of(pair * HEAD_DIM, HEAD_DIM)
    low_ref[pl.ds(query_width + place, HEAD_DIM), :] = keys
    low_ref[pl.ds(query_width + kv_width + place, HEAD_DIM), :] = values
    key_rows = keys.T
    for head in range(GROUP):
        rows = slice(head * HEAD_DIM, (head + 1) * HEAD_DIM)
        queries = rotate(q_ref[rows, :], cos_table, sine_table).astype(jnp.bfloat16)
        low_ref[pl.ds(pl.multiple_of((pair * GROUP + head) * HEAD_DIM, HEAD_DIM), HEAD_DIM), :] = (
            queries
        )
        scaled = queries * HEAD_DIM ** (-0.5)
        for start in range(0, SEQ, TILE):
            size = start + TILE
            scores = dot(key_rows[:size], scaled[:, start:size]) + bias[:size, start:size]
            summit = jnp.max(scores, axis=0, keepdims=True)
            powers = jnp.exp(scores - summit)
            totals = jnp.sum(powers, axis=0, keepdims=True)
            blended = dot(values[:, :size], powers.astype(jnp.bfloat16)) / totals
            out_ref[rows, start:size] = blended.astype(jnp.bfloat16)
            log_ref[0, head : head + 1, start:size] = summit + jnp.log(totals)


def attend_back_kernel(
    q_ref,
    k_ref,
    v_ref,
    grad_ref,
    log_ref,
    cos_ref,
    sin_ref,
    seg_row,
    seg_col,
    out_ref,
    bias,
    key_total,
    value_total,
):
    fill_bias(bias, seg_row, seg_col)
    pair = pl.program_id(0)
    cos_table = cos_ref[...]
    sine_table = -sin_ref[...]
    scale = HEAD_DIM ** (-0.5)
    keys = k_ref[...]
    key_rows = keys.T
    value_rows = v_ref[...].T
    key_total[...] = jnp.zeros_like(key_total)
    value_total[...] = jnp.zeros_like(value_total)
    for head in range(GROUP):
        rows = slice(head * HEAD_DIM, (head + 1) * HEAD_DIM)
        queries = q_ref[rows, :]
        scaled = queries * scale
        query_rows = scaled.T
        incoming = grad_ref[rows, :]
        incoming_rows = incoming.T
        parts = []
        for start in range(0, SEQ, TILE):
            size = start + TILE
            scores = dot(key_rows[:size], scaled[:, start:size]) + bias[:size, start:size]
            chances = jnp.exp(scores - log_ref[0, head : head + 1, start:size])
            chance_grad = dot(value_rows[:size], incoming[:, start:size])
            centre = jnp.sum(chances * chance_grad, axis=0, keepdims=True)
            score_grad = (chances * (chance_grad - centre)).astype(jnp.bfloat16)
            parts.append(dot(keys[:, :size], score_grad) * scale)
            key_total[:size] += dot(score_grad, query_rows[start:size])
            value_total[:size] += dot(chances.astype(jnp.bfloat16), incoming_rows[start:size])
        query_grad = rotate(jnp.concatenate(parts, axis=1), cos_table, sine_table)
        out_ref[pl.ds(pl.multiple_of((pair * GROUP + head) * HEAD_DIM, HEAD_DIM), HEAD_DIM), :] = (
            query_grad.astype(jnp.bfloat16)
        )
    query_width = HEADS * HEAD_DIM
    kv_width = KV_HEADS * HEAD_DIM
    place = pl.multiple_of(pair * HEAD_DIM, HEAD_DIM)
    key_grad = rotate(key_total[...].T, cos_table, sine_table)
    out_ref[pl.ds(query_width + place, HEAD_DIM), :] = key_grad.astype(jnp.bfloat16)
    out_ref[pl.ds(query_width + kv_width + place, HEAD_DIM), :] = (
        value_total[...].T.astype(jnp.bfloat16)
    )


def whole_spec(*shape):
    return pl.BlockSpec(shape, lambda step: (0,) * len(shape))


def head_specs():
    return [
        pl.BlockSpec((GROUP * HEAD_DIM, SEQ), lambda j: (j, 0)),
        pl.BlockSpec((HEAD_DIM, SEQ), lambda j: (HEADS + j, 0)),
        pl.BlockSpec((HEAD_DIM, SEQ), lambda j: (HEADS + KV_HEADS + j, 0)),
    ]


def attend(projected, cos_table, sine_table, segments):
    half_dim = HEAD_DIM // 2
    width = projected.shape[0]
    return pl.pallas_call(
        attend_kernel,
        grid=(KV_HEADS,),
        in_specs=head_specs()
        + [
            whole_spec(half_dim, SEQ),
            whole_spec(half_dim, SEQ),
            whole_spec(1, SEQ),
            whole_spec(SEQ, 1),
        ],
        out_specs=[
            whole_spec(width, SEQ),
            pl.BlockSpec((GROUP * HEAD_DIM, SEQ), lambda j: (j, 0)),
            pl.BlockSpec((1, GROUP, SEQ), lambda j: (j, 0, 0)),
        ],
        out_shape=[
            jax.ShapeDtypeStruct((width, SEQ), jnp.bfloat16),
            jax.ShapeDtypeStruct((HEADS * HEAD_DIM, SEQ), jnp.bfloat16),
            jax.ShapeDtypeStruct((KV_HEADS, GROUP, SEQ), jnp.float32),
        ],
        scratch_shapes=[pltpu.VMEM((SEQ, SEQ), jnp.float32)],
        compiler_params=pltpu.CompilerParams(vmem_limit_bytes=48 << 20),
        cost_estimate=pl.CostEstimate(
            flops=20 * SEQ * SEQ * HEADS * HEAD_DIM,
            bytes_accessed=16 << 20,
            transcendentals=HEADS * SEQ * SEQ,
        ),
        name="attend",
    )(
        projected,
        projected,
        projected,
        cos_table,
        sine_table,
        segments.reshape(1, SEQ),
        segments.reshape(SEQ, 1),
    )


def attend_back(low, blended_grad, log_totals, cos_table, sine_table, segments):
    half_dim = HEAD_DIM // 2
    width = low.shape[0]
    return pl.pallas_call(
        attend_back_kernel,
        grid=(KV_HEADS,),
        in_specs=head_specs()
        + [
            pl.BlockSpec((GROUP * HEAD_DIM, SEQ), lambda j: (j, 0)),
            pl.BlockSpec((1, GROUP, SEQ), lambda j: (j, 0, 0)),
            whole_spec(half_dim, SEQ),
            whole_spec(half_dim, SEQ),
            whole_spec(1, SEQ),
            whole_spec(SEQ, 1),
        ],
        out_specs=whole_spec(width, SEQ),
        out_shape=jax.ShapeDtypeStruct((width, SEQ), jnp.bfloat16),
        scratch_shapes=[
            pltpu.VMEM((SEQ, SEQ), jnp.float32),
            pltpu.VMEM((SEQ, HEAD_DIM), jnp.float32),
            pltpu.VMEM((SEQ, HEAD_DIM), jnp.float32),
        ],
        compiler_params=pltpu.CompilerParams(vmem_limit_bytes=48 << 20),
        cost_estimate=pl.CostEstimate(
            flops=60 * SEQ * SEQ * HEADS * HEAD_DIM,
            bytes_accessed=16 << 20,
            transcendentals=HEADS * SEQ * SEQ,
        ),
        name="attend_back",
    )(
        low,
        low,
        low,
        blended_grad,
        log_totals,
        cos_table,
        sine_table,
        segments.reshape(1, SEQ),
        segments.reshape(SEQ, 1),
    )


def mlp_kernel(
    normed_ref,
    normed_turned,
    back_ref,
    back_turned,
    pair_ref,
    down_ref,
    out_ref,
    grad_ref,
    pair_out,
    down_out,
    hidden_keep,
    gate_keep,
    up_keep,
):
    first = pl.program_id(0) == 0
    height = pair_ref.shape[0] * pair_ref.shape[3]
    width = pair_ref.shape[4]
    token_count = normed_ref.shape[0]

    @pl.when(first)
    def _():
        out_ref[...] = jnp.zeros_like(out_ref)
        grad_ref[...] = jnp.zeros_like(grad_ref)

    gate_weight = pair_ref[:, 0, 0].reshape(height, width)
    up_weight = pair_ref[:, 0, 1].reshape(height, width)
    down_weight = down_ref[:, 0].reshape(height, width)

    def forward(step, carry):
        rows = pl.ds(pl.multiple_of(step * TILE, TILE), TILE)
        normed = normed_ref[rows, :]
        gate_pre = dot(normed, gate_weight)
        up_pre = dot(normed, up_weight)
        hidden_grad = dot(back_ref[rows, :], down_weight)
        sigmoid_gate = 1.0 / (1.0 + jnp.exp(-gate_pre))
        silu_gate = gate_pre * sigmoid_gate
        hidden = (silu_gate * up_pre).astype(jnp.bfloat16)
        gate_grad = (
            hidden_grad * up_pre * sigmoid_gate * (1.0 + gate_pre * (1.0 - sigmoid_gate))
        ).astype(jnp.bfloat16)
        up_grad = (hidden_grad * silu_gate).astype(jnp.bfloat16)
        hidden_keep[rows, :] = hidden
        gate_keep[rows, :] = gate_grad
        up_keep[rows, :] = up_grad
        out_ref[rows, :] += dot(hidden, down_weight, ((1,), (1,)))
        grad_ref[rows, :] += dot(gate_grad, gate_weight, ((1,), (1,))) + dot(
            up_grad, up_weight, ((1,), (1,))
        )
        return carry

    lax.fori_loop(0, token_count // TILE, forward, 0)
    block_rows = pair_ref.shape[3]
    for block in range(pair_ref.shape[0]):
        rows = slice(block * block_rows, (block + 1) * block_rows)
        left = normed_turned[rows, :]
        pair_out[block, 0, 0] = dot(left, gate_keep[...]).astype(jnp.bfloat16)
        pair_out[block, 0, 1] = dot(left, up_keep[...]).astype(jnp.bfloat16)
        down_out[block, 0] = dot(back_turned[rows, :], hidden_keep[...]).astype(jnp.bfloat16)


def mlp(normed, back, pair_grid, down_grid):
    token_count, features = normed.shape
    row_count, col_count, _, height, width = pair_grid.shape
    aligned = height % 16 == 0 and width % 128 == 0
    if not aligned:
        units = col_count * width
        pieces = units // 640
        pair_grid = pair_grid.transpose(2, 0, 3, 1, 4).reshape(1, 2, features, pieces, 640)
        pair_grid = pair_grid.transpose(0, 3, 1, 2, 4)
        down_grid = down_grid.transpose(0, 2, 1, 3).reshape(1, features, pieces, 640)
        down_grid = down_grid.transpose(0, 2, 1, 3)
    rows, cols, _, tall, wide = pair_grid.shape
    single = pl.Buffered(1)

    def fixed(*shape):
        return pl.BlockSpec(shape, lambda c: (0, 0), pipeline_mode=single)

    pair_spec = pl.BlockSpec((rows, 1, 2, tall, wide), lambda c: (0, c, 0, 0, 0))
    down_spec = pl.BlockSpec((rows, 1, tall, wide), lambda c: (0, c, 0, 0))
    outs = pl.pallas_call(
        mlp_kernel,
        grid=(cols,),
        in_specs=[
            fixed(token_count, features),
            fixed(features, token_count),
            fixed(token_count, features),
            fixed(features, token_count),
            pair_spec,
            down_spec,
        ],
        out_specs=[
            fixed(token_count, features),
            fixed(token_count, features),
            pair_spec,
            down_spec,
        ],
        out_shape=[
            jax.ShapeDtypeStruct((token_count, features), jnp.float32),
            jax.ShapeDtypeStruct((token_count, features), jnp.float32),
            jax.ShapeDtypeStruct(pair_grid.shape, jnp.bfloat16),
            jax.ShapeDtypeStruct(down_grid.shape, jnp.bfloat16),
        ],
        scratch_shapes=[pltpu.VMEM((token_count, wide), jnp.bfloat16)] * 3,
        compiler_params=pltpu.CompilerParams(vmem_limit_bytes=58 << 20),
        cost_estimate=pl.CostEstimate(
            flops=18 * token_count * features * cols * wide,
            bytes_accessed=64 << 20,
            transcendentals=token_count * cols * wide,
        ),
        name="mlp",
    )(normed, normed.T, back, back.T, pair_grid, down_grid)
    mlp_out, normed_grad, pair_grad, down_grad = outs
    if not aligned:
        pair_grad = pair_grad.transpose(0, 2, 3, 1, 4).reshape(
            2, row_count, height, col_count, width
        )
        pair_grad = pair_grad.transpose(1, 3, 0, 2, 4)
        down_grad = down_grad.transpose(0, 2, 1, 3).reshape(row_count, height, col_count, width)
        down_grad = down_grad.transpose(0, 2, 1, 3)
    return mlp_out, normed_grad, pair_grad, down_grad


def from_grid(stack, row_count, col_count):
    _, height, width = stack.shape
    shaped = stack.reshape(row_count, col_count, height, width).transpose(0, 2, 1, 3)
    return shaped.reshape(row_count * height, col_count * width)


def into_grid(whole, row_count, col_count):
    height = whole.shape[0] // row_count
    width = whole.shape[1] // col_count
    shaped = whole.reshape(row_count, height, col_count, width).transpose(0, 2, 1, 3)
    return shaped.reshape(row_count * col_count, height, width)


def norm_backward(inputs, inverse, scales, incoming):
    weighted = incoming * scales
    gain_part = jnp.sum(incoming * inputs * inverse, axis=0)
    input_part = inverse * weighted - inputs * inverse**3 * jnp.mean(
        weighted * inputs, axis=-1, keepdims=True
    )
    return (gain_part, input_part)


def adam_step(weight, gradient, moment, square, step_rate, decay_factor):
    moment_new = beta_one * moment + (1.0 - beta_one) * gradient
    square_new = beta_two * square + (1.0 - beta_two) * gradient * gradient
    scaled_step = (
        moment_new
        / (1.0 - beta_one**STEP)
        / (jnp.sqrt(square_new / (1.0 - beta_two**STEP)) + adam_eps)
    )
    return (moment_new, square_new, weight - step_rate * (scaled_step + decay_factor * weight))


def shards(
    hidden_in,
    cotangent,
    segment_ids,
    positions,
    query_weight,
    key_weight,
    value_weight,
    output_weight,
    gate_up_weight,
    down_weight,
    norm_gains,
    query_moment,
    key_moment,
    value_moment,
    output_moment,
    gate_up_moment,
    down_moment,
    gains_moment,
    query_square,
    key_square,
    value_square,
    output_square,
    gate_up_square,
    down_square,
    gains_square,
):
    row_count = lax.axis_size("row")
    col_count = lax.axis_size("col")
    query_part = query_weight.shape[1]
    key_part = key_weight.shape[1]
    cuts = (query_part, query_part + key_part, query_part + 2 * key_part)
    query_width = HEADS * HEAD_DIM
    kv_width = KV_HEADS * HEAD_DIM

    def gather(block):
        return lax.all_gather(block[None], ("row", "col"), axis=0, tiled=True)

    def scatter(stack):
        return lax.psum_scatter(stack, ("row", "col"), scatter_dimension=0, tiled=True)[0]

    def total(part):
        return lax.psum(part, "dp").astype(jnp.float32)

    first_stack = gather(
        jnp.concatenate([query_weight, key_weight, value_weight, output_weight], axis=1).astype(
            jnp.bfloat16
        )
    )
    gate_up_stack = gather(gate_up_weight.astype(jnp.bfloat16))
    down_stack = gather(down_weight.astype(jnp.bfloat16))
    first_low = jnp.concatenate(
        [
            from_grid(first_stack[:, :, : cuts[0]], row_count, col_count),
            from_grid(first_stack[:, :, cuts[0] : cuts[1]], row_count, col_count),
            from_grid(first_stack[:, :, cuts[1] : cuts[2]], row_count, col_count),
        ],
        axis=1,
    )
    output_low = from_grid(first_stack[:, :, cuts[2] :], row_count, col_count)
    gate_up_grid = gate_up_stack.reshape((row_count, col_count) + gate_up_weight.shape)
    down_grid = down_stack.reshape((row_count, col_count) + down_weight.shape)

    cos_table, sine_table = rope_tables(positions)
    inputs = hidden_in.astype(jnp.float32)
    inverse_one = lax.rsqrt(jnp.mean(inputs * inputs, axis=-1, keepdims=True) + norm_eps)
    normed_one = (inputs * inverse_one * norm_gains[0]).astype(jnp.bfloat16)
    projected = dot(first_low, normed_one, ((0,), (1,)))
    low, blended, log_totals = attend(projected, cos_table, sine_table, segment_ids)
    middle = inputs + dot(blended, output_low, ((0,), (0,)))
    inverse_two = lax.rsqrt(jnp.mean(middle * middle, axis=-1, keepdims=True) + norm_eps)
    normed_two = (middle * inverse_two * norm_gains[1]).astype(jnp.bfloat16)
    mlp_out, normed_two_grad, gate_up_block, down_block = mlp(
        normed_two, cotangent, gate_up_grid, down_grid
    )
    gate_up_part = scatter(gate_up_block.reshape(gate_up_stack.shape))
    down_part = scatter(down_block.reshape(down_stack.shape))
    block_out = (middle + mlp_out).astype(jnp.bfloat16)
    gain_two, middle_part = norm_backward(middle, inverse_two, norm_gains[1], normed_two_grad)
    middle_grad = cotangent.astype(jnp.float32) + middle_part
    middle_low = middle_grad.astype(jnp.bfloat16)
    output_block = dot(blended, middle_low, ((1,), (0,))).astype(jnp.bfloat16)
    blended_grad = dot(output_low, middle_low, ((1,), (1,))).astype(jnp.bfloat16)
    projected_grad = attend_back(
        low, blended_grad, log_totals, cos_table, sine_table, segment_ids
    )
    projected_grad, gate_up_part, down_part = lax.optimization_barrier(
        (projected_grad, gate_up_part, down_part)
    )
    gate_up_sum = total(gate_up_part)
    down_sum = total(down_part)
    first_block = dot(normed_one, projected_grad, ((0,), (1,))).astype(jnp.bfloat16)
    first_part = scatter(
        jnp.concatenate(
            [
                into_grid(first_block[:, :query_width], row_count, col_count),
                into_grid(
                    first_block[:, query_width : query_width + kv_width], row_count, col_count
                ),
                into_grid(first_block[:, query_width + kv_width :], row_count, col_count),
                into_grid(output_block, row_count, col_count),
            ],
            axis=2,
        )
    )
    first_part, gate_up_sum, down_sum = lax.optimization_barrier(
        (first_part, gate_up_sum, down_sum)
    )
    first_sum = total(first_part)
    normed_one_grad = dot(projected_grad, first_low, ((0,), (1,)))
    gain_one, input_part = norm_backward(inputs, inverse_one, norm_gains[0], normed_one_grad)
    input_grad = (middle_grad + input_part).astype(jnp.bfloat16)
    reduced = (
        first_sum[:, : cuts[0]],
        first_sum[:, cuts[0] : cuts[1]],
        first_sum[:, cuts[1] : cuts[2]],
        first_sum[:, cuts[2] :],
        gate_up_sum,
        down_sum,
    )
    gains_grad = lax.psum(jnp.stack([gain_one, gain_two]), ("dp", "row", "col"))
    query_update = adam_step(
        query_weight, reduced[0], query_moment, query_square, matrix_rate, decay_rate
    )
    key_update = adam_step(key_weight, reduced[1], key_moment, key_square, matrix_rate, decay_rate)
    value_update = adam_step(
        value_weight, reduced[2], value_moment, value_square, matrix_rate, decay_rate
    )
    output_update = adam_step(
        output_weight, reduced[3], output_moment, output_square, matrix_rate, decay_rate
    )
    gate_up_update = adam_step(
        gate_up_weight, reduced[4], gate_up_moment, gate_up_square, matrix_rate, decay_rate
    )
    down_update = adam_step(
        down_weight, reduced[5], down_moment, down_square, matrix_rate, decay_rate
    )
    gains_update = adam_step(norm_gains, gains_grad, gains_moment, gains_square, gain_rate, 0.0)
    return (
        block_out,
        input_grad,
        reduced[0],
        query_update[0],
        query_update[1],
        query_update[2],
        reduced[1],
        key_update[0],
        key_update[1],
        key_update[2],
        reduced[2],
        value_update[0],
        value_update[1],
        value_update[2],
        reduced[3],
        output_update[0],
        output_update[1],
        output_update[2],
        reduced[4],
        gate_up_update[0],
        gate_up_update[1],
        gate_up_update[2],
        reduced[5],
        down_update[0],
        down_update[1],
        down_update[2],
        gains_grad,
        gains_update[0],
        gains_update[1],
        gains_update[2],
    )


def solution(mesh):
    in_specs = (
        P(("dp", "row", "col"), None),
        P(("dp", "row", "col"), None),
        P(("dp", "row", "col")),
        P(("dp", "row", "col")),
        P("row", "col"),
        P("row", "col"),
        P("row", "col"),
        P("row", "col"),
        P(None, "row", "col"),
        P("row", "col"),
        P(),
        P("row", "col"),
        P("row", "col"),
        P("row", "col"),
        P("row", "col"),
        P(None, "row", "col"),
        P("row", "col"),
        P(),
        P("row", "col"),
        P("row", "col"),
        P("row", "col"),
        P("row", "col"),
        P(None, "row", "col"),
        P("row", "col"),
        P(),
    )
    out_specs = (
        P(("dp", "row", "col"), None),
        P(("dp", "row", "col"), None),
        P("row", "col"),
        P("row", "col"),
        P("row", "col"),
        P("row", "col"),
        P("row", "col"),
        P("row", "col"),
        P("row", "col"),
        P("row", "col"),
        P("row", "col"),
        P("row", "col"),
        P("row", "col"),
        P("row", "col"),
        P("row", "col"),
        P("row", "col"),
        P("row", "col"),
        P("row", "col"),
        P(None, "row", "col"),
        P(None, "row", "col"),
        P(None, "row", "col"),
        P(None, "row", "col"),
        P("row", "col"),
        P("row", "col"),
        P("row", "col"),
        P("row", "col"),
        P(),
        P(),
        P(),
        P(),
    )
    return jax.shard_map(shards, mesh=mesh, in_specs=in_specs, out_specs=out_specs, check_vma=False)
```
